32 devices in a mesh: row: 8 (over z, core), col: 4 (over y, x).
Axes of the slice: x: 2, y: 2, z: 4, core: 2. Of those that a mesh axis runs over, the one named last changes fastest.
Arguments:
- clean_in: bfloat16 [512, 8192], P('row', 'col'), may hold values from -6 to 6
- corrupt_in: bfloat16 [512, 8192], P('row', 'col'), may hold values from -6 to 6
- patch_mask: int32 [512], replicated, may hold values 0 or 1
- gate_weight: bfloat16 [8192, 28672], P('col', 'row'), may hold values from -0.0625 to 0.0625
- up_weight: bfloat16 [8192, 28672], P('col', 'row'), may hold values from -0.0625 to 0.0625
- down_weight: bfloat16 [28672, 8192], P('row', 'col'), may hold values from -0.03125 to 0.03125
Outputs:
- clean_out: float32 [512, 8192], P('row', 'col')
- patched_out: float32 [512, 8192], P('row', 'col')
The draws below stay inside these ranges and needn't reach their ends.
All inputs are finite; a program needn't handle non-finite values.
Results may differ from the reference program's by a relative error of at most 0.0029.
Values may be sent and summed in bfloat16 or wider, within the bound.
No kernel may reach another device: no remote copies, remote signals or barrier semaphores. Data moves between devices by JAX's collectives and lax.ppermute only.
A program may use at most 128 MiB of HBM per device.

```python
import jax
import jax.numpy as jnp

D = 8192
FF = 28672
TOK = 512


def set_ends(entries, key, smallest, largest):
    place = [jax.random.randint(jax.random.fold_in(key, axis), (), 0, length) for axis, length in enumerate(entries.shape)]
    widest = entries.shape.index(max(entries.shape))
    beside = place[:widest] + [(place[widest] + 1) % entries.shape[widest]] + place[widest + 1:]
    return entries.at[tuple(place)].set(smallest).at[tuple(beside)].set(largest)


def level_of(rng, extent, shards, low, high):
    gain, own = 1.0, jax.random.fold_in(rng, 6)
    for dim, parts in shards:
        heights = jnp.exp(jax.random.uniform(jax.random.fold_in(own, dim), (parts,), jnp.float32, low / len(shards), high / len(shards)))
        gain = gain * jnp.repeat(heights, extent[dim] // parts).reshape([-1 if axis == dim else 1 for axis in range(len(extent))])
    return gain


def bell_draw(own_key, dims, width, most, shards=(), dtype=jnp.bfloat16):
    array = width * jax.random.normal(own_key, dims, jnp.float32)
    if shards:
        array = array * level_of(own_key, dims, shards, -0.22, 0.18)
    return jnp.clip(array, -most, most).astype(dtype)


def setup_inputs(seed: int = 0) -> dict:
    streams_of = jax.random.split(jax.random.key(seed), 7)
    clean_in = bell_draw(streams_of[0], (TOK, D), 1.0, 6.0, ((0, 8), (1, 4)))
    corrupt_in = bell_draw(streams_of[1], (TOK, D), 1.0, 6.0, ((0, 8), (1, 4)))
    patch_mask = set_ends((jax.random.randint(streams_of[2], (TOK,), 0, 2) < 1).astype(jnp.int32), jax.random.fold_in(streams_of[2], 1), 0, 1)
    gate_weight = bell_draw(streams_of[3], (D, FF), D ** -0.5, 0.0625, ((0, 4), (1, 8)))
    up_weight = bell_draw(streams_of[4], (D, FF), D ** -0.5, 0.0625, ((0, 4), (1, 8)))
    down_weight = bell_draw(streams_of[5], (FF, D), FF ** -0.5, 0.03125, ((0, 8), (1, 4)))
    return dict(clean_in=clean_in, corrupt_in=corrupt_in, patch_mask=patch_mask, gate_weight=gate_weight, up_weight=up_weight, down_weight=down_weight)


def hidden_of(inputs, gate_weight, up_weight):
    gate_part = jnp.dot(inputs, gate_weight, preferred_element_type=jnp.float32)
    up_part = jnp.dot(inputs, up_weight, preferred_element_type=jnp.float32)
    return (jax.nn.silu(gate_part) * up_part).astype(jnp.bfloat16)


def reference(clean_in, corrupt_in, patch_mask, gate_weight, up_weight, down_weight):
    hidden_clean = hidden_of(clean_in, gate_weight, up_weight)
    hidden_corrupt = hidden_of(corrupt_in, gate_weight, up_weight)
    hidden_patched = jnp.where(patch_mask[:, None] == 1, hidden_clean, hidden_corrupt)
    clean_out = jnp.dot(hidden_clean, down_weight, preferred_element_type=jnp.float32)
    patched_out = jnp.dot(hidden_patched, down_weight, preferred_element_type=jnp.float32)
    return (clean_out, patched_out)
```

```python
import jax
import jax.numpy as jnp
from jax import lax
from jax.experimental import pallas as pl
from jax.experimental.pallas import tpu as pltpu
from jax.sharding import PartitionSpec as P

BF16 = jnp.bfloat16
F32 = jnp.float32
I16 = jnp.int16
I32 = jnp.int32
LN2 = 0.6931471805599453
LANES = 128
VMEM_LIMIT = 52 * 1024 * 1024
COST = 25_000_000_000


def dot(a, b):
    return jnp.dot(a, b, preferred_element_type=F32)


def dot_first(a, b):
    return lax.dot_general(a, b, (((0,), (0,)), ((), ())), preferred_element_type=F32)


def tile_of(width, sizes):
    for t in sizes:
        if width % t == 0:
            return t
    raise ValueError(width)


def col_tile(width):
    return tile_of(width, (512, 896, 256, 128))


def in_vmem(n):
    return [pl.BlockSpec(memory_space=pltpu.VMEM)] * n


def in_place(n):
    return [pl.BlockSpec(memory_space=pl.ANY)] * n


def in_smem():
    return [pl.BlockSpec(memory_space=pltpu.SMEM)]


def call(kernel, in_specs, out_shape, args, scratch=()):
    return pl.pallas_call(
        kernel,
        in_specs=in_specs,
        out_specs=jax.tree.map(lambda _: pl.BlockSpec(memory_space=pltpu.VMEM), out_shape),
        out_shape=out_shape,
        scratch_shapes=list(scratch),
        compiler_params=pltpu.CompilerParams(vmem_limit_bytes=VMEM_LIMIT),
        cost_estimate=pl.CostEstimate(flops=COST, bytes_accessed=1_000_000, transcendentals=0),
    )(*args)


def natural(rows, n_col, reverse, c):
    blk, bits = rows // n_col, n_col.bit_length() - 1
    i = lax.broadcasted_iota(I32, (rows, 1), 0)
    rel = sum((i >= b * blk).astype(I32) for b in range(1, n_col))
    inside = i - rel * blk
    if reverse:
        rel = sum(((rel >> b) & 1) << (bits - 1 - b) for b in range(bits))
    return (rel ^ c) * blk + inside


def encode(value):
    top = jnp.max(jnp.abs(value), axis=1, keepdims=True)
    power = jnp.floor(14.0 - jnp.log(jnp.maximum(top, 1e-30)) * (1.0 / LN2))
    return jnp.round(value * jnp.exp(power * LN2)).astype(I32).astype(I16), power


def decode(ref, cols, factor):
    return ref[:, cols].astype(I32).astype(F32) * factor


def factors_of(ref, width):
    return jnp.exp(ref[:, width:].astype(I32).astype(F32) * -LN2)


def sums_shape(half, width):
    return [jax.ShapeDtypeStruct((half, width + LANES), I16), jax.ShapeDtypeStruct((half, width), F32)]


def corrupt_labels(row, q, own, mask, after=()):
    tok = mask.shape[0]
    shift = q.bit_length() - 1

    def kernel(row_ref, mask_ref, *refs):
        out_ref = refs[-1]
        s = lax.broadcasted_iota(I32, (tok, tok), 0)
        t = lax.broadcasted_iota(I32, (tok, tok), 1)
        source = (((t >> shift) ^ row_ref[0]) << shift) + (t & (q - 1))
        hot = jnp.where(s == source, 1.0, 0.0).astype(BF16)
        need = jnp.broadcast_to(jnp.where(mask_ref[...] == 1, 0.0, 1.0), (8, tok)).astype(BF16)
        need = dot(need, hot)
        before = (s < t) & ((s < own) == (t < own))
        rank = dot(need.astype(BF16), jnp.where(before, 1.0, 0.0).astype(BF16))
        first = jnp.where(lax.broadcasted_iota(I32, (8, tok), 1) < own, own, 0)
        out_ref[...] = jnp.where(need > 0.5, rank.astype(I32) + first, -1)

    out = call(
        kernel,
        in_smem() + in_vmem(1) + in_place(len(after)),
        jax.ShapeDtypeStruct((8, tok), I32),
        (row, mask[None, :], *after),
    )
    return out[0]


def first_sum(c, n_col, reverse, chunk, weight, after):
    rows, label, sources = chunk
    depth, width = weight.shape
    half, tile = rows // 2, col_tile(width)
    tiles, n = width // tile, len(sources)

    def kernel(c_ref, label_ref, *refs):
        src_refs, w_ref = refs[:n], refs[n]
        send_ref, keep_ref, buf, sem = refs[-4:]

        def copy(t):
            return pltpu.make_async_copy(w_ref.at[:, pl.ds(t * tile, tile)], buf.at[t], sem.at[t])

        for t in range(tiles):
            copy(t).start()
        pos = natural(rows, n_col, reverse, c_ref[0])
        hot = jnp.where(label_ref[...] == pos, 1.0, 0.0).astype(BF16)
        x = dot(hot, jnp.concatenate([r[...] for r in src_refs], axis=0)).astype(BF16)
        lane = lax.broadcasted_iota(I32, (half, LANES), 1)
        powers = jnp.zeros((half, LANES), F32)
        for t in range(tiles):
            cols = slice(t * tile, (t + 1) * tile)
            copy(t).wait()
            product = dot(x, buf[t])
            keep_ref[:, cols] = product[:half]
            digits, power = encode(product[half:])
            send_ref[:, cols] = digits
            powers = jnp.where(lane == t, power, powers)
        send_ref[:, width:] = powers.astype(I32).astype(I16)

    return call(
        kernel,
        in_smem() + in_vmem(1 + n) + in_place(1 + len(after)),
        sums_shape(half, width),
        (c, label[None, :], *sources, weight, *after),
        (pltpu.VMEM((tiles, depth, tile), BF16), pltpu.SemaphoreType.DMA((tiles,))),
    )


def next_sum(keep, recv, after):
    rows, width = keep.shape
    half, tile = rows // 2, col_tile(width)

    def kernel(keep_ref, recv_ref, *refs):
        send_ref, out_ref = refs[len(after) :]
        factors = factors_of(recv_ref, width)
        powers = jnp.zeros((half, LANES), F32)
        lane = lax.broadcasted_iota(I32, powers.shape, 1)
        for t in range(width // tile):
            cols = slice(t * tile, (t + 1) * tile)
            total = keep_ref[:, cols] + decode(recv_ref, cols, factors[:, t : t + 1])
            out_ref[:, cols] = total[:half]
            digits, power = encode(total[half:])
            send_ref[:, cols] = digits
            powers = jnp.where(lane == t, power, powers)
        send_ref[:, width:] = powers.astype(I32).astype(I16)

    return call(kernel, in_vmem(2) + in_place(len(after)), sums_shape(half, width), (keep, recv, *after))


def activation(gate_keep, gate_recv, up_keep, up_recv, after):
    rows, width = gate_keep.shape
    tile = col_tile(width)

    def kernel(gk_ref, gr_ref, uk_ref, ur_ref, *refs):
        out_ref = refs[-1]
        gate_f, up_f = factors_of(gr_ref, width), factors_of(ur_ref, width)
        for t in range(width // tile):
            cols = slice(t * tile, (t + 1) * tile)
            gate = gk_ref[:, cols] + decode(gr_ref, cols, gate_f[:, t : t + 1])
            up = uk_ref[:, cols] + decode(ur_ref, cols, up_f[:, t : t + 1])
            out_ref[:, cols] = (gate * (1.0 / (1.0 + jnp.exp(-gate))) * up).astype(BF16)

    return call(
        kernel,
        in_vmem(4) + in_place(len(after)),
        jax.ShapeDtypeStruct((rows, width), BF16),
        (gate_keep, gate_recv, up_keep, up_recv, *after),
    )


def down(c, n_col, pieces, weight, after):
    rows = pieces[0][0].shape[0]
    width, model = weight.shape
    depth = tile_of(width, (896, 512, 256, 128))
    steps, half = width // depth, rows // 2
    n_in = len(pieces) * (1 + n_col)

    def kernel(c_ref, *refs):
        ins, w_ref = refs[:n_in], refs[n_in]
        keep_ref, send_ref, buf, sem = refs[-4:]

        def copy(t):
            return pltpu.make_async_copy(w_ref.at[pl.ds(t * depth, depth)], buf.at[t], sem.at[t])

        for t in range(steps):
            copy(t).start()
        hots = []
        for i, (_, blocks) in enumerate(pieces):
            pos = natural(n_col * blocks[0].shape[0], n_col, False, c_ref[0])
            hots.append(jnp.where(ins[i * (1 + n_col)][...] == pos, 1.0, 0.0).astype(BF16))
        for t in range(steps):
            h = None
            for i in range(len(pieces)):
                block_refs = ins[i * (1 + n_col) + 1 : (i + 1) * (1 + n_col)]
                cols = slice(t * depth, (t + 1) * depth)
                have = jnp.concatenate([r[:, cols].astype(F32) for r in block_refs], axis=0).astype(BF16)
                part = dot_first(hots[i], have)
                h = part if h is None else h + part
            copy(t).wait()
            part = dot(h.astype(BF16), buf[t])
            if t == 0:
                keep_ref[...] = part[:half]
                send_ref[...] = part[half:]
            else:
                keep_ref[...] += part[:half]
                send_ref[...] += part[half:]

    args = []
    for want, blocks in pieces:
        args += [want[None, :], *blocks]
    return call(
        kernel,
        in_smem() + in_vmem(n_in) + in_place(1 + len(after)),
        [jax.ShapeDtypeStruct((half, model), F32)] * 2,
        (c, *args, weight, *after),
        (pltpu.VMEM((steps, depth, model), BF16), pltpu.SemaphoreType.DMA((steps,))),
    )


def round_up(n, m):
    return -(-n // m) * m


def capacities(tok, chip_tok, full):
    if full:
        return chip_tok, tok - chip_tok
    own = min(round_up(chip_tok + chip_tok * 3 // 4, 32) - chip_tok, chip_tok)
    rest = min(round_up((tok - chip_tok) * 7 // 12, 32), tok - chip_tok)
    return own, rest


def body(full, n_row, n_col, clean_in, corrupt_in, patch_mask, gate_weight, up_weight, down_weight):
    bits = n_col.bit_length() - 1
    col = lax.axis_index("col").astype(I32)[None]
    row = lax.axis_index("row").astype(I32)[None]
    tok, q = patch_mask.shape[0], clean_in.shape[0]
    chip_tok, chips = 2 * q, n_row // 2
    cap_own, cap_rest = capacities(tok, chip_tok, full)

    def swap_col(a, mask):
        return lax.ppermute(a, "col", [(i, i ^ mask) for i in range(n_col)])

    def swap_row(a, mask):
        return lax.ppermute(a, "row", [(i, i ^ mask) for i in range(n_row)])

    last = []

    def ran(out):
        last[:] = [jax.tree.leaves(out)[0]]
        return out

    def gate_up(chunk):
        return [
            list(ran(first_sum(col, n_col, reverse, chunk, weight, tuple(last))))
            for reverse, weight in ((True, gate_weight), (False, up_weight))
        ]

    def exchange(state, step):
        return [swap_col(s[0], 1 << bit) for s, bit in zip(state, (step, bits - 1 - step))]

    def sums(state, recvs):
        for s, recv in zip(state, recvs):
            s[0], s[1] = ran(next_sum(s[1], recv, tuple(last)))

    def act(state, recvs):
        return ran(activation(state[0][1], recvs[0], state[1][1], recvs[1], tuple(last)))

    def project(pieces):
        return ran(down(col, n_col, pieces, down_weight, tuple(last)))

    def blocks_of(h):
        return [h] + [swap_col(h, m) for m in range(1, n_col)]

    def from_chips(x, first):
        out = []
        for d in range(first, chips):
            mine = swap_row(x, 2 * d) if d else x
            out.append([mine, swap_row(mine, 1)])
        return out

    ((clean_0, clean_1),) = [[clean_in, swap_row(clean_in, 1)]]
    corrupt_0, corrupt_1 = corrupt_in, swap_row(corrupt_in, 1)
    labels = ran(corrupt_labels(row, q, chip_tok, patch_mask))
    i_own = jnp.arange(chip_tok, dtype=I32)
    own = (
        chip_tok + cap_own,
        jnp.concatenate([i_own, labels[:chip_tok]]),
        [clean_0, clean_1, corrupt_0, corrupt_1],
    )
    corrupt_rest = from_chips(corrupt_in, 1)
    rest = (cap_rest, labels[chip_tok:], [x for pair in corrupt_rest for x in pair])
    clean_rest = from_chips(clean_in, 1)

    def clean_chunk(first, end):
        rows = (end - first) * chip_tok
        return rows, jnp.arange(rows, dtype=I32), [x for pair in clean_rest[first - 1 : end - 1] for x in pair]

    spans = ([(2, chips)] if chips > 2 else []) + [(1, 2)]
    chunks = [own, rest] + [clean_chunk(*s) for s in spans]

    def want_own(lab):
        corrupt = jnp.where(lab < 0, i_own, lab)
        return jnp.concatenate([i_own[:q], corrupt[:q], i_own[q:], corrupt[q:]])

    def wants(lab, first, end):
        n = end - first
        lab = lab.reshape(chips - 1, 2, q)[first - 1 : end - 1].transpose(1, 0, 2)
        o, d, i = (lax.broadcasted_iota(I32, (2, n, q), k) for k in range(3))
        p = (d * 2 + o) * q + i
        none = jnp.full_like(p, -1)
        clean = jnp.stack([p, jnp.where(lab < 0, p, none)], axis=2).reshape(-1)
        corrupt = jnp.stack([none, lab], axis=2).reshape(-1)
        return clean, corrupt

    def send_home(keep, send, first, end):
        both = (keep + swap_row(send, 1)).astype(BF16).reshape(end - first, chip_tok, -1)
        return [swap_row(both[d - first], 2 * d) for d in range(first, end)]

    n = len(chunks)
    states, recvs, hidden = [None] * n, [None] * n, [None] * n
    parts = None
    late = None
    for tick in range(n + bits):
        for phase in [0] + list(range(1, bits + 1)):
            k = tick - phase
            if not 0 <= k < n:
                continue
            if phase == 0:
                states[k] = gate_up(chunks[k])
            elif phase < bits:
                sums(states[k], recvs[k])
            else:
                hidden[k] = blocks_of(act(states[k], recvs[k]))
            if phase < bits:
                recvs[k] = exchange(states[k], phase)
        if late is None and hidden[0] is not None:
            late = ran(corrupt_labels(row, q, chip_tok, patch_mask, tuple(last)))
        elif parts is None and hidden[1] is not None:
            keep, send = project([(want_own(late[:chip_tok]), hidden[0])])
            parts = [keep, swap_row(send, 1)]
    for k, (first, end) in enumerate(spans):
        w_clean, w_rest = wants(late[chip_tok:], first, end)
        keep, send = project([(w_clean, hidden[2 + k]), (w_rest, hidden[1])])
        parts += send_home(keep, send, first, end)

    def total(rows):
        out = parts[0][rows]
        for p in parts[1:]:
            out = out + p[rows].astype(F32)
        return out

    return total(slice(0, q)), total(slice(q, 2 * q))


def solution(mesh):
    n_row, n_col = mesh.shape["row"], mesh.shape["col"]
    placed = (
        P("row", "col"),
        P("row", "col"),
        P(),
        P("col", "row"),
        P("col", "row"),
        P("row", "col"),
    )

    def on_device(*args):
        patch_mask = args[2]
        tok = patch_mask.shape[0]
        chip_tok = 2 * args[0].shape[0]
        cap_own, cap_rest = capacities(tok, chip_tok, False)
        per_chip = jnp.sum((patch_mask != 1).astype(I32).reshape(tok // chip_tok, chip_tok), axis=1)
        fits = (jnp.max(per_chip) <= cap_own) & (jnp.sum(per_chip) - jnp.min(per_chip) <= cap_rest)
        outs = body(False, n_row, n_col, *args)
        return lax.cond(fits, lambda *a: outs, lambda *a: body(True, n_row, n_col, *a), *args)

    return jax.shard_map(
        on_device,
        mesh=mesh,
        in_specs=placed,
        out_specs=(P("row", "col"), P("row", "col")),
        check_vma=False,
    )
```

```python
import jax
import jax.numpy as jnp
from jax import lax
from jax.experimental import pallas as pl
from jax.experimental.pallas import tpu as pltpu
from jax.sharding import PartitionSpec as P

BF16 = jnp.bfloat16
F32 = jnp.float32
I16 = jnp.int16
I32 = jnp.int32
LN2 = 0.6931471805599453
LANES = 128
VMEM_LIMIT = 52 * 1024 * 1024
COST_PER_US = 300_000_000


def dot(a, b):
    return jnp.dot(a, b, preferred_element_type=F32)


def dot_first(a, b):
    return lax.dot_general(a, b, (((0,), (0,)), ((), ())), preferred_element_type=F32)


def tile_of(width, sizes):
    for t in sizes:
        if width % t == 0:
            return t
    raise ValueError(width)


def col_tile(width):
    return tile_of(width, (512, 896, 256, 128))


def in_vmem(n):
    return [pl.BlockSpec(memory_space=pltpu.VMEM)] * n


def in_place(n):
    return [pl.BlockSpec(memory_space=pl.ANY)] * n


def in_smem():
    return [pl.BlockSpec(memory_space=pltpu.SMEM)]


def call(kernel, in_specs, out_shape, args, scratch=(), us=2):
    return pl.pallas_call(
        kernel,
        in_specs=in_specs,
        out_specs=jax.tree.map(lambda _: pl.BlockSpec(memory_space=pltpu.VMEM), out_shape),
        out_shape=out_shape,
        scratch_shapes=list(scratch),
        compiler_params=pltpu.CompilerParams(vmem_limit_bytes=VMEM_LIMIT),
        cost_estimate=pl.CostEstimate(flops=us * COST_PER_US, bytes_accessed=1_000_000, transcendentals=0),
    )(*args)


def natural(rows, n_col, reverse, c):
    blk, bits = rows // n_col, n_col.bit_length() - 1
    i = lax.broadcasted_iota(I32, (rows, 1), 0)
    rel = sum((i >= b * blk).astype(I32) for b in range(1, n_col))
    inside = i - rel * blk
    if reverse:
        rel = sum(((rel >> b) & 1) << (bits - 1 - b) for b in range(bits))
    return (rel ^ c) * blk + inside


def encode(value):
    top = jnp.max(jnp.abs(value), axis=1, keepdims=True)
    power = jnp.floor(14.0 - jnp.log(jnp.maximum(top, 1e-30)) * (1.0 / LN2))
    return jnp.round(value * jnp.exp(power * LN2)).astype(I32).astype(I16), power


def decode(ref, cols, factor):
    return ref[:, cols].astype(I32).astype(F32) * factor


def factors_of(ref, width):
    return jnp.exp(ref[:, width:].astype(I32).astype(F32) * -LN2)


def sums_shape(half, width):
    return [jax.ShapeDtypeStruct((half, width + LANES), I16), jax.ShapeDtypeStruct((half, width), F32)]


def held(x, *after):
    def kernel(*_):
        pass

    return pl.pallas_call(
        kernel,
        in_specs=in_place(1 + len(after)),
        out_specs=in_place(1)[0],
        out_shape=jax.ShapeDtypeStruct(x.shape, x.dtype),
        input_output_aliases={0: 0},
        cost_estimate=pl.CostEstimate(flops=1, bytes_accessed=1, transcendentals=0),
    )(x, *after)


def corrupt_labels(row, q, own, mask, after=()):
    tok = mask.shape[0]
    shift = q.bit_length() - 1

    def kernel(row_ref, mask_ref, *refs):
        out_ref = refs[-1]
        s = lax.broadcasted_iota(I32, (tok, tok), 0)
        t = lax.broadcasted_iota(I32, (tok, tok), 1)
        source = (((t >> shift) ^ row_ref[0]) << shift) + (t & (q - 1))
        hot = jnp.where(s == source, 1.0, 0.0).astype(BF16)
        need = jnp.broadcast_to(jnp.where(mask_ref[...] == 1, 0.0, 1.0), (8, tok)).astype(BF16)
        need = dot(need, hot)
        before = (s < t) & ((s < own) == (t < own))
        rank = dot(need.astype(BF16), jnp.where(before, 1.0, 0.0).astype(BF16))
        first = jnp.where(lax.broadcasted_iota(I32, (8, tok), 1) < own, own, 0)
        out_ref[...] = jnp.where(need > 0.5, rank.astype(I32) + first, -1)

    out = call(
        kernel,
        in_smem() + in_vmem(1) + in_place(len(after)),
        jax.ShapeDtypeStruct((8, tok), I32),
        (row, mask[None, :], *after),
    )
    return out[0]


def first_sum(c, n_col, reverse, chunk, weight, after):
    rows, label, sources = chunk
    depth, width = weight.shape
    half, tile = rows // 2, col_tile(width)
    tiles, n = width // tile, len(sources)

    def kernel(c_ref, label_ref, *refs):
        src_refs, w_ref = refs[:n], refs[n]
        send_ref, keep_ref, buf, sem = refs[-4:]

        def copy(t):
            return pltpu.make_async_copy(w_ref.at[:, pl.ds(t * tile, tile)], buf.at[t], sem.at[t])

        for t in range(tiles):
            copy(t).start()
        pos = natural(rows, n_col, reverse, c_ref[0])
        hot = jnp.where(label_ref[...] == pos, 1.0, 0.0).astype(BF16)
        x = dot(hot, jnp.concatenate([r[...] for r in src_refs], axis=0)).astype(BF16)
        lane = lax.broadcasted_iota(I32, (half, LANES), 1)
        powers = jnp.zeros((half, LANES), F32)
        for t in range(tiles):
            cols = slice(t * tile, (t + 1) * tile)
            copy(t).wait()
            product = dot(x, buf[t])
            keep_ref[:, cols] = product[:half]
            digits, power = encode(product[half:])
            send_ref[:, cols] = digits
            powers = jnp.where(lane == t, power, powers)
        send_ref[:, width:] = powers.astype(I32).astype(I16)

    return call(
        kernel,
        in_smem() + in_vmem(1 + n) + in_place(1 + len(after)),
        sums_shape(half, width),
        (c, label[None, :], *sources, weight, *after),
        (pltpu.VMEM((tiles, depth, tile), BF16), pltpu.SemaphoreType.DMA((tiles,))),
        us=9,
    )


def next_sum(keep, recv, after):
    rows, width = keep.shape
    half, tile = rows // 2, col_tile(width)

    def kernel(keep_ref, recv_ref, *refs):
        send_ref, out_ref = refs[len(after) :]
        factors = factors_of(recv_ref, width)
        powers = jnp.zeros((half, LANES), F32)
        lane = lax.broadcasted_iota(I32, powers.shape, 1)
        for t in range(width // tile):
            cols = slice(t * tile, (t + 1) * tile)
            total = keep_ref[:, cols] + decode(recv_ref, cols, factors[:, t : t + 1])
            out_ref[:, cols] = total[:half]
            digits, power = encode(total[half:])
            send_ref[:, cols] = digits
            powers = jnp.where(lane == t, power, powers)
        send_ref[:, width:] = powers.astype(I32).astype(I16)

    return call(kernel, in_vmem(2) + in_place(len(after)), sums_shape(half, width), (keep, recv, *after))


def activation(gate_keep, gate_recv, up_keep, up_recv, after):
    rows, width = gate_keep.shape
    tile = col_tile(width)

    def kernel(gk_ref, gr_ref, uk_ref, ur_ref, *refs):
        out_ref = refs[-1]
        gate_f, up_f = factors_of(gr_ref, width), factors_of(ur_ref, width)
        for t in range(width // tile):
            cols = slice(t * tile, (t + 1) * tile)
            gate = gk_ref[:, cols] + decode(gr_ref, cols, gate_f[:, t : t + 1])
            up = uk_ref[:, cols] + decode(ur_ref, cols, up_f[:, t : t + 1])
            out_ref[:, cols] = (gate * (1.0 / (1.0 + jnp.exp(-gate))) * up).astype(BF16)

    return call(
        kernel,
        in_vmem(4) + in_place(len(after)),
        jax.ShapeDtypeStruct((rows, width), BF16),
        (gate_keep, gate_recv, up_keep, up_recv, *after),
    )


def down(c, n_col, pieces, weight, after):
    rows = pieces[0][0].shape[0]
    width, model = weight.shape
    depth = tile_of(width, (896, 512, 256, 128))
    steps, half = width // depth, rows // 2
    n_in = len(pieces) * (1 + n_col)

    def kernel(c_ref, *refs):
        ins, w_ref = refs[:n_in], refs[n_in]
        keep_ref, send_ref, buf, sem = refs[-4:]

        def copy(t):
            return pltpu.make_async_copy(w_ref.at[pl.ds(t * depth, depth)], buf.at[t], sem.at[t])

        for t in range(steps):
            copy(t).start()
        hots = []
        for i, (_, blocks) in enumerate(pieces):
            pos = natural(n_col * blocks[0].shape[0], n_col, False, c_ref[0])
            hots.append(jnp.where(ins[i * (1 + n_col)][...] == pos, 1.0, 0.0).astype(BF16))
        for t in range(steps):
            h = None
            for i in range(len(pieces)):
                block_refs = ins[i * (1 + n_col) + 1 : (i + 1) * (1 + n_col)]
                cols = slice(t * depth, (t + 1) * depth)
                have = jnp.concatenate([r[:, cols].astype(F32) for r in block_refs], axis=0).astype(BF16)
                part = dot_first(hots[i], have)
                h = part if h is None else h + part
            copy(t).wait()
            part = dot(h.astype(BF16), buf[t])
            if t == 0:
                keep_ref[...] = part[:half]
                send_ref[...] = part[half:]
            else:
                keep_ref[...] += part[:half]
                send_ref[...] += part[half:]

    args = []
    for want, blocks in pieces:
        args += [want[None, :], *blocks]
    return call(
        kernel,
        in_smem() + in_vmem(n_in) + in_place(1 + len(after)),
        [jax.ShapeDtypeStruct((half, model), F32)] * 2,
        (c, *args, weight, *after),
        (pltpu.VMEM((steps, depth, model), BF16), pltpu.SemaphoreType.DMA((steps,))),
        us=9,
    )


def add_up(clean, patched, us):
    shape = jax.ShapeDtypeStruct(clean[0].shape, F32)
    n = len(clean)

    def kernel(*refs):
        for out_ref, ins in ((refs[-2], refs[:n]), (refs[-1], refs[n:-2])):
            out = ins[0][...].astype(F32)
            for r in ins[1:]:
                out = out + r[...].astype(F32)
            out_ref[...] = out

    return tuple(call(kernel, in_vmem(n + len(patched)), [shape, shape], (*clean, *patched), us=us))


def round_up(n, m):
    return -(-n // m) * m


def capacities(tok, chip_tok, full):
    if full:
        return chip_tok, tok - chip_tok
    own = min(round_up(chip_tok + chip_tok * 3 // 4, 32) - chip_tok, chip_tok)
    rest = min(round_up((tok - chip_tok) * 7 // 12, 32), tok - chip_tok)
    return own, rest


def body(full, n_row, n_col, clean_in, corrupt_in, patch_mask, gate_weight, up_weight, down_weight):
    bits = n_col.bit_length() - 1
    col = lax.axis_index("col").astype(I32)[None]
    row = lax.axis_index("row").astype(I32)[None]
    tok, q = patch_mask.shape[0], clean_in.shape[0]
    chip_tok, chips = 2 * q, n_row // 2
    cap_own, cap_rest = capacities(tok, chip_tok, full)

    def swap_col(a, mask):
        return lax.ppermute(a, "col", [(i, i ^ mask) for i in range(n_col)])

    def swap_row(a, mask):
        return lax.ppermute(a, "row", [(i, i ^ mask) for i in range(n_row)])

    last = []

    def ran(out):
        last[:] = [jax.tree.leaves(out)[0]]
        return out

    def gate_up(chunk):
        return [
            list(ran(first_sum(col, n_col, reverse, chunk, weight, tuple(last))))
            for reverse, weight in ((True, gate_weight), (False, up_weight))
        ]

    def exchange(state, step):
        return [swap_col(s[0], 1 << bit) for s, bit in zip(state, (step, bits - 1 - step))]

    def sums(state, recvs):
        for s, recv in zip(state, recvs):
            s[0], s[1] = ran(next_sum(s[1], recv, tuple(last)))

    def act(state, recvs):
        return ran(activation(state[0][1], recvs[0], state[1][1], recvs[1], tuple(last)))

    def project(pieces):
        return ran(down(col, n_col, pieces, down_weight, tuple(last)))

    def blocks_of(h):
        return [h] + [swap_col(h, m) for m in range(1, n_col)]

    clean_0, clean_1 = clean_in, swap_row(clean_in, 1)
    corrupt_0, corrupt_1 = corrupt_in, swap_row(corrupt_in, 1)
    labels = ran(corrupt_labels(row, q, chip_tok, patch_mask))
    i_own = jnp.arange(chip_tok, dtype=I32)
    own = (
        chip_tok + cap_own,
        jnp.concatenate([i_own, labels[:chip_tok]]),
        [clean_0, clean_1, corrupt_0, corrupt_1],
    )
    def both_cores(arrived):
        out = []
        for x in arrived:
            x = held(x, last[0])
            out += [x, swap_row(x, 1)]
        return out

    def from_chips(x, first, end):
        return [swap_row(x, 2 * d) for d in range(first, end)]

    def want_own(lab):
        corrupt = jnp.where(lab < 0, i_own, lab)
        return jnp.concatenate([i_own[:q], corrupt[:q], i_own[q:], corrupt[q:]])

    def by_core(x, first, end):
        return x.reshape(-1, 2, q)[first - 1 : end - 1].transpose(1, 0, 2)

    def wants(lab, first, end):
        clean = by_core(jnp.arange((chips - 1) * chip_tok, dtype=I32), first, end) - (first - 1) * chip_tok
        lab = by_core(lab, first, end)
        return clean, jnp.where(lab < 0, clean, -1), lab

    sent = []

    def send_home(keep, send, first, end):
        both = (keep + swap_row(send, 1)).astype(BF16)
        sent[:] = [both]
        return [swap_row(x, 2 * (first + j)) for j, x in enumerate(jnp.split(both, end - first))]

    near = (1, 2)
    spans = {"far": (2, chips), "near": near} if chips > 2 else {"near": near}
    names = ["own", "far", "rest", "near"] if chips > 2 else ["own", "rest", "near"]
    n = len(names)
    arrived = {}
    if chips > 2:
        arrived["far"] = from_chips(clean_in, 2, chips)
    arrived["rest"] = from_chips(corrupt_in, 1, chips) if chips == 2 else None

    def chunk_of(name):
        if name == "own":
            return own
        if name == "rest":
            return cap_rest, labels[chip_tok:], both_cores(arrived[name])
        first, end = spans[name]
        rows = (end - first) * chip_tok
        return rows, jnp.arange(rows, dtype=I32), both_cores(arrived[name])

    states, recvs, hidden = {}, {}, {}
    parts = [[], []]

    def project_own():
        late = ran(corrupt_labels(row, q, chip_tok, patch_mask, tuple(last)))
        keep, send = project([(want_own(late[:chip_tok]), hidden["own"])])
        recv = swap_row(send, 1)
        for run in (0, 1):
            rows = slice(run * q, (run + 1) * q)
            parts[run] += [keep[rows], recv[rows]]
        return late[chip_tok:]

    def project_far_clean(lab):
        clean, _, _ = wants(lab, *spans["far"])
        keep, send = project([(clean.reshape(-1), hidden["far"])])
        parts[0].extend(send_home(keep, send, *spans["far"]))

    def project_far_patched(lab):
        _, patched, corrupt = wants(lab, *spans["far"])
        keep, send = project([(patched.reshape(-1), hidden["far"]), (corrupt.reshape(-1), hidden["rest"])])
        send = held(send, *parts[0][2:])
        parts[1].extend(send_home(keep, send, *spans["far"]))

    def project_near(lab):
        clean, patched, corrupt = wants(lab, *near)
        none = jnp.full_like(clean, -1)
        want_clean = jnp.concatenate([clean, patched], axis=1).reshape(-1)
        want_corrupt = jnp.concatenate([none, corrupt], axis=1).reshape(-1)
        keep, send = project([(want_clean, hidden["near"]), (want_corrupt, hidden["rest"])])
        (both,) = send_home(keep, send, *near)
        parts[0].append(both[:q])
        parts[1].append(both[q:])

    lab = None
    for tick in range(n + bits):
        order = [0, *range(bits, 0, -1)] if tick < n else [*range(1, bits + 1)]
        for phase in order:
            k = tick - phase
            if not 0 <= k < n:
                continue
            name = names[k]
            if phase == 0:
                states[name] = gate_up(chunk_of(name))
            elif phase < bits:
                if k >= 2:
                    last.extend(hidden.get(names[k - 2], ())[1:])
                sums(states[name], recvs[name])
            else:
                hidden[name] = blocks_of(act(states[name], recvs[name]))
            if phase < bits:
                recvs[name] = exchange(states[name], phase)
            if phase == 0 and k + 2 < n and "rest" == names[k + (2 if chips > 2 else 1)]:
                arrived["rest"] = from_chips(corrupt_in, 1, chips)
            if phase == 0 and names[min(k + 2, n - 1)] == "near" and "near" not in arrived:
                arrived["near"] = from_chips(held(clean_in, last[0]), *near)
        if lab is None and "own" in hidden and tick >= bits + 1:
            lab = project_own()
        elif "far" in hidden and not parts[1][2:] and len(parts[0]) == 2 and tick >= bits + 2:
            project_far_clean(lab)
    if chips > 2:
        last.extend(sent)
        project_far_patched(lab)
    project_near(lab)

    return add_up(*parts, 2)


def solution(mesh):
    n_row, n_col = mesh.shape["row"], mesh.shape["col"]
    placed = (
        P("row", "col"),
        P("row", "col"),
        P(),
        P("col", "row"),
        P("col", "row"),
        P("row", "col"),
    )

    def on_device(*args):
        patch_mask = args[2]
        tok = patch_mask.shape[0]
        chip_tok = 2 * args[0].shape[0]
        cap_own, cap_rest = capacities(tok, chip_tok, False)
        per_chip = jnp.sum((patch_mask != 1).astype(I32).reshape(tok // chip_tok, chip_tok), axis=1)
        fits = (jnp.max(per_chip) <= cap_own) & (jnp.sum(per_chip) - jnp.min(per_chip) <= cap_rest)
        outs = body(False, n_row, n_col, *args)
        return lax.cond(fits, lambda *a: outs, lambda *a: body(True, n_row, n_col, *a), *args)

    return jax.shard_map(
        on_device,
        mesh=mesh,
        in_specs=placed,
        out_specs=(P("row", "col"), P("row", "col")),
        check_vma=False,
    )
```

```python
import jax
import jax.numpy as jnp
from jax import lax
from jax.experimental import pallas as pl
from jax.experimental.pallas import tpu as pltpu
from jax.sharding import PartitionSpec as P

BF16 = jnp.bfloat16
F32 = jnp.float32
I16 = jnp.int16
I32 = jnp.int32
LN2 = 0.6931471805599453
LANES = 128
VMEM_LIMIT = 52 * 1024 * 1024
COST_PER_US = 300_000_000


def dot(a, b):
    return jnp.dot(a, b, preferred_element_type=F32)


def dot_first(a, b):
    return lax.dot_general(a, b, (((0,), (0,)), ((), ())), preferred_element_type=F32)


def tile_of(width, sizes):
    for t in sizes:
        if width % t == 0:
            return t
    raise ValueError(width)


def col_tile(width):
    return tile_of(width, (512, 896, 256, 128))


def in_vmem(n):
    return [pl.BlockSpec(memory_space=pltpu.VMEM)] * n


def in_place(n):
    return [pl.BlockSpec(memory_space=pl.ANY)] * n


def in_smem():
    return [pl.BlockSpec(memory_space=pltpu.SMEM)]


def call(kernel, in_specs, out_shape, args, scratch=(), us=2):
    return pl.pallas_call(
        kernel,
        in_specs=in_specs,
        out_specs=jax.tree.map(lambda _: pl.BlockSpec(memory_space=pltpu.VMEM), out_shape),
        out_shape=out_shape,
        scratch_shapes=list(scratch),
        compiler_params=pltpu.CompilerParams(vmem_limit_bytes=VMEM_LIMIT),
        cost_estimate=pl.CostEstimate(flops=us * COST_PER_US, bytes_accessed=1_000_000, transcendentals=0),
    )(*args)


def natural(rows, n_col, reverse, c):
    blk, bits = rows // n_col, n_col.bit_length() - 1
    i = lax.broadcasted_iota(I32, (rows, 1), 0)
    rel = sum((i >= b * blk).astype(I32) for b in range(1, n_col))
    inside = i - rel * blk
    if reverse:
        rel = sum(((rel >> b) & 1) << (bits - 1 - b) for b in range(bits))
    return (rel ^ c) * blk + inside


def encode(value):
    top = jnp.max(jnp.abs(value), axis=1, keepdims=True)
    power = jnp.floor(14.0 - jnp.log(jnp.maximum(top, 1e-30)) * (1.0 / LN2))
    return jnp.round(value * jnp.exp(power * LN2)).astype(I32).astype(I16), power


def decode(ref, cols, factor):
    return ref[:, cols].astype(I32).astype(F32) * factor


def factors_of(ref, width):
    return jnp.exp(ref[:, width:].astype(I32).astype(F32) * -LN2)


def sums_shape(half, width):
    return [jax.ShapeDtypeStruct((half, width + LANES), I16), jax.ShapeDtypeStruct((half, width), F32)]


def held(x, *after):
    def kernel(*_):
        pass

    return pl.pallas_call(
        kernel,
        in_specs=in_place(1 + len(after)),
        out_specs=in_place(1)[0],
        out_shape=jax.ShapeDtypeStruct(x.shape, x.dtype),
        input_output_aliases={0: 0},
        cost_estimate=pl.CostEstimate(flops=1, bytes_accessed=1, transcendentals=0),
    )(x, *after)


def corrupt_labels(row, q, own, mask, after=()):
    tok = mask.shape[0]
    shift = q.bit_length() - 1

    def kernel(row_ref, mask_ref, *refs):
        out_ref = refs[-1]
        s = lax.broadcasted_iota(I32, (tok, tok), 0)
        t = lax.broadcasted_iota(I32, (tok, tok), 1)
        source = (((t >> shift) ^ row_ref[0]) << shift) + (t & (q - 1))
        hot = jnp.where(s == source, 1.0, 0.0).astype(BF16)
        need = jnp.broadcast_to(jnp.where(mask_ref[...] == 1, 0.0, 1.0), (8, tok)).astype(BF16)
        need = dot(need, hot)
        before = (s < t) & ((s < own) == (t < own))
        rank = dot(need.astype(BF16), jnp.where(before, 1.0, 0.0).astype(BF16))
        first = jnp.where(lax.broadcasted_iota(I32, (8, tok), 1) < own, own, 0)
        out_ref[...] = jnp.where(need > 0.5, rank.astype(I32) + first, -1)

    out = call(
        kernel,
        in_smem() + in_vmem(1) + in_place(len(after)),
        jax.ShapeDtypeStruct((8, tok), I32),
        (row, mask[None, :], *after),
    )
    return out[0]


def first_sum(c, n_col, reverse, chunk, weight, after):
    rows, label, sources = chunk
    depth, width = weight.shape
    half, tile = rows // 2, col_tile(width)
    tiles, n = width // tile, len(sources)

    def kernel(c_ref, label_ref, *refs):
        src_refs, w_ref = refs[:n], refs[n]
        send_ref, keep_ref, buf, sem = refs[-4:]

        def copy(t):
            return pltpu.make_async_copy(w_ref.at[:, pl.ds(t * tile, tile)], buf.at[t], sem.at[t])

        for t in range(tiles):
            copy(t).start()
        pos = natural(rows, n_col, reverse, c_ref[0])
        hot = jnp.where(label_ref[...] == pos, 1.0, 0.0).astype(BF16)
        x = dot(hot, jnp.concatenate([r[...] for r in src_refs], axis=0)).astype(BF16)
        lane = lax.broadcasted_iota(I32, (half, LANES), 1)
        powers = jnp.zeros((half, LANES), F32)
        for t in range(tiles):
            cols = slice(t * tile, (t + 1) * tile)
            copy(t).wait()
            product = dot(x, buf[t])
            keep_ref[:, cols] = product[:half]
            digits, power = encode(product[half:])
            send_ref[:, cols] = digits
            powers = jnp.where(lane == t, power, powers)
        send_ref[:, width:] = powers.astype(I32).astype(I16)

    return call(
        kernel,
        in_smem() + in_vmem(1 + n) + in_place(1 + len(after)),
        sums_shape(half, width),
        (c, label[None, :], *sources, weight, *after),
        (pltpu.VMEM((tiles, depth, tile), BF16), pltpu.SemaphoreType.DMA((tiles,))),
        us=9,
    )


def next_sum(keep, recv, after):
    rows, width = keep.shape
    half, tile = rows // 2, col_tile(width)

    def kernel(keep_ref, recv_ref, *refs):
        send_ref, out_ref = refs[len(after) :]
        factors = factors_of(recv_ref, width)
        powers = jnp.zeros((half, LANES), F32)
        lane = lax.broadcasted_iota(I32, powers.shape, 1)
        for t in range(width // tile):
            cols = slice(t * tile, (t + 1) * tile)
            total = keep_ref[:, cols] + decode(recv_ref, cols, factors[:, t : t + 1])
            out_ref[:, cols] = total[:half]
            digits, power = encode(total[half:])
            send_ref[:, cols] = digits
            powers = jnp.where(lane == t, power, powers)
        send_ref[:, width:] = powers.astype(I32).astype(I16)

    return call(kernel, in_vmem(2) + in_place(len(after)), sums_shape(half, width), (keep, recv, *after))


def activation(gate_keep, gate_recv, up_keep, up_recv, after):
    rows, width = gate_keep.shape
    tile = col_tile(width)

    def kernel(gk_ref, gr_ref, uk_ref, ur_ref, *refs):
        out_ref = refs[-1]
        gate_f, up_f = factors_of(gr_ref, width), factors_of(ur_ref, width)
        for t in range(width // tile):
            cols = slice(t * tile, (t + 1) * tile)
            gate = gk_ref[:, cols] + decode(gr_ref, cols, gate_f[:, t : t + 1])
            up = uk_ref[:, cols] + decode(ur_ref, cols, up_f[:, t : t + 1])
            out_ref[:, cols] = (gate * (1.0 / (1.0 + jnp.exp(-gate))) * up).astype(BF16)

    return call(
        kernel,
        in_vmem(4) + in_place(len(after)),
        jax.ShapeDtypeStruct((rows, width), BF16),
        (gate_keep, gate_recv, up_keep, up_recv, *after),
    )


def down(c, n_col, pieces, weight, after):
    rows = pieces[0][0].shape[0]
    width, model = weight.shape
    depth = tile_of(width, (896, 512, 256, 128))
    steps, half = width // depth, rows // 2
    n_in = len(pieces) * (1 + n_col)

    def kernel(c_ref, *refs):
        ins, w_ref = refs[:n_in], refs[n_in]
        keep_ref, send_ref, buf, sem = refs[-4:]

        def copy(t):
            return pltpu.make_async_copy(w_ref.at[pl.ds(t * depth, depth)], buf.at[t], sem.at[t])

        for t in range(steps):
            copy(t).start()
        hots = []
        for i, (_, blocks) in enumerate(pieces):
            pos = natural(n_col * blocks[0].shape[0], n_col, False, c_ref[0])
            hots.append(jnp.where(ins[i * (1 + n_col)][...] == pos, 1.0, 0.0).astype(BF16))
        for t in range(steps):
            h = None
            for i in range(len(pieces)):
                block_refs = ins[i * (1 + n_col) + 1 : (i + 1) * (1 + n_col)]
                cols = slice(t * depth, (t + 1) * depth)
                have = jnp.concatenate([r[:, cols].astype(F32) for r in block_refs], axis=0).astype(BF16)
                part = dot_first(hots[i], have)
                h = part if h is None else h + part
            copy(t).wait()
            part = dot(h.astype(BF16), buf[t])
            if t == 0:
                keep_ref[...] = part[:half]
                send_ref[...] = part[half:]
            else:
                keep_ref[...] += part[:half]
                send_ref[...] += part[half:]

    args = []
    for want, blocks in pieces:
        args += [want[None, :], *blocks]
    return call(
        kernel,
        in_smem() + in_vmem(n_in) + in_place(1 + len(after)),
        [jax.ShapeDtypeStruct((half, model), F32)] * 2,
        (c, *args, weight, *after),
        (pltpu.VMEM((steps, depth, model), BF16), pltpu.SemaphoreType.DMA((steps,))),
        us=9,
    )


def add_up(clean, patched, us):
    shape = jax.ShapeDtypeStruct(clean[0].shape, F32)
    n = len(clean)

    def kernel(*refs):
        for out_ref, ins in ((refs[-2], refs[:n]), (refs[-1], refs[n:-2])):
            out = ins[0][...].astype(F32)
            for r in ins[1:]:
                out = out + r[...].astype(F32)
            out_ref[...] = out

    return tuple(call(kernel, in_vmem(n + len(patched)), [shape, shape], (*clean, *patched), us=us))


def round_up(n, m):
    return -(-n // m) * m


def capacities(tok, chip_tok, full):
    if full:
        return chip_tok, tok - chip_tok
    own = min(round_up(chip_tok + chip_tok * 3 // 4, 32) - chip_tok, chip_tok)
    rest = min(round_up((tok - chip_tok) * 7 // 12, 32), tok - chip_tok)
    return own, rest


def body(full, n_row, n_col, clean_in, corrupt_in, patch_mask, gate_weight, up_weight, down_weight):
    bits = n_col.bit_length() - 1
    col = lax.axis_index("col").astype(I32)[None]
    row = lax.axis_index("row").astype(I32)[None]
    tok, q = patch_mask.shape[0], clean_in.shape[0]
    chip_tok, chips = 2 * q, n_row // 2
    cap_own, cap_rest = capacities(tok, chip_tok, full)

    def swap_col(a, mask):
        return lax.ppermute(a, "col", [(i, i ^ mask) for i in range(n_col)])

    def swap_row(a, mask):
        return lax.ppermute(a, "row", [(i, i ^ mask) for i in range(n_row)])

    last = []

    def ran(out):
        last[:] = [jax.tree.leaves(out)[0]]
        return out

    def gate_up(chunk):
        return [
            list(ran(first_sum(col, n_col, reverse, chunk, weight, tuple(last))))
            for reverse, weight in ((True, gate_weight), (False, up_weight))
        ]

    def exchange(state, step):
        return [swap_col(s[0], 1 << bit) for s, bit in zip(state, (step, bits - 1 - step))]

    def sums(state, recvs):
        for s, recv in zip(state, recvs):
            s[0], s[1] = ran(next_sum(s[1], recv, tuple(last)))

    def act(state, recvs):
        return ran(activation(state[0][1], recvs[0], state[1][1], recvs[1], tuple(last)))

    def project(pieces):
        return ran(down(col, n_col, pieces, down_weight, tuple(last)))

    def blocks_of(h):
        return [h] + [swap_col(h, m) for m in range(1, n_col)]

    clean_0, clean_1 = clean_in, swap_row(clean_in, 1)
    corrupt_0, corrupt_1 = corrupt_in, swap_row(corrupt_in, 1)
    labels = ran(corrupt_labels(row, q, chip_tok, patch_mask))
    i_own = jnp.arange(chip_tok, dtype=I32)
    own = (
        chip_tok + cap_own,
        jnp.concatenate([i_own, labels[:chip_tok]]),
        [clean_0, clean_1, corrupt_0, corrupt_1],
    )
    def both_cores(arrived):
        out = []
        for x in arrived:
            x = held(x, last[0])
            out += [x, swap_row(x, 1)]
        return out

    def from_chips(x, first, end):
        return [swap_row(x, 2 * d) for d in range(first, end)]

    def want_own(lab):
        corrupt = jnp.where(lab < 0, i_own, lab)
        return jnp.concatenate([i_own[:q], corrupt[:q], i_own[q:], corrupt[q:]])

    def by_core(x, first, end):
        return x.reshape(-1, 2, q)[first - 1 : end - 1].transpose(1, 0, 2)

    def wants(lab, first, end):
        clean = by_core(jnp.arange((chips - 1) * chip_tok, dtype=I32), first, end) - (first - 1) * chip_tok
        lab = by_core(lab, first, end)
        return clean, jnp.where(lab < 0, clean, -1), lab

    sent = []

    def send_home(keep, send, first, end):
        both = (keep + swap_row(send, 1)).astype(BF16)
        sent[:] = [both]
        return [swap_row(x, 2 * (first + j)) for j, x in enumerate(jnp.split(both, end - first))]

    near = (1, 2)
    spans = {"far": (2, chips), "near": near} if chips > 2 else {"near": near}
    names = ["own", "far", "rest", "near"] if chips > 2 else ["own", "rest", "near"]
    n = len(names)
    arrived = {}
    if chips > 2:
        arrived["far"] = from_chips(clean_in, 2, chips)
    arrived["rest"] = from_chips(corrupt_in, 1, chips) if chips == 2 else None

    def chunk_of(name):
        if name == "own":
            return own
        if name == "rest":
            return cap_rest, labels[chip_tok:], both_cores(arrived[name])
        first, end = spans[name]
        rows = (end - first) * chip_tok
        return rows, jnp.arange(rows, dtype=I32), both_cores(arrived[name])

    states, recvs, hidden = {}, {}, {}
    parts = [[], []]

    def project_own(late):
        keep, send = project([(want_own(late[:chip_tok]), hidden["own"])])
        recv = swap_row(held(send, *parts[0], *parts[1]), 1)
        for run in (0, 1):
            rows = slice(run * q, (run + 1) * q)
            parts[run] += [keep[rows], recv[rows]]

    def project_far_clean(lab):
        clean, _, _ = wants(lab, *spans["far"])
        keep, send = project([(clean.reshape(-1), hidden["far"])])
        parts[0].extend(send_home(keep, send, *spans["far"]))

    def project_far_patched(lab):
        _, patched, corrupt = wants(lab, *spans["far"])
        keep, send = project([(patched.reshape(-1), hidden["far"]), (corrupt.reshape(-1), hidden["rest"])])
        send = held(send, *parts[0])
        parts[1].extend(send_home(keep, send, *spans["far"]))

    def project_near(lab):
        clean, patched, corrupt = wants(lab, *near)
        none = jnp.full_like(clean, -1)
        want_clean = jnp.concatenate([clean, patched], axis=1).reshape(-1)
        want_corrupt = jnp.concatenate([none, corrupt], axis=1).reshape(-1)
        keep, send = project([(want_clean, hidden["near"]), (want_corrupt, hidden["rest"])])
        (both,) = send_home(keep, send, *near)
        parts[0].append(both[:q])
        parts[1].append(both[q:])

    lab = None
    for tick in range(n + bits):
        order = [0, *range(bits, 0, -1)] if tick < n else [*range(1, bits + 1)]
        for phase in order:
            k = tick - phase
            if not 0 <= k < n:
                continue
            name = names[k]
            if phase == 0:
                states[name] = gate_up(chunk_of(name))
            elif phase < bits:
                if k >= 2:
                    last.extend(hidden.get(names[k - 2], ())[1:])
                sums(states[name], recvs[name])
            else:
                hidden[name] = act(states[name], recvs[name])
                if name != "own":
                    hidden[name] = blocks_of(hidden[name])
            if phase < bits:
                recvs[name] = exchange(states[name], phase)
            if phase == 0 and k + 2 < n and "rest" == names[k + (2 if chips > 2 else 1)]:
                arrived["rest"] = from_chips(corrupt_in, 1, chips)
            if phase == 0 and names[min(k + 2, n - 1)] == "near" and "near" not in arrived:
                arrived["near"] = from_chips(held(clean_in, last[0]), *near)
        if lab is None and "own" in hidden and tick >= bits + 1:
            late = ran(corrupt_labels(row, q, chip_tok, patch_mask, tuple(last)))
            lab = late[chip_tok:]
        elif "far" in hidden and not parts[1][2:] and not parts[0] and tick >= bits + 2:
            project_far_clean(lab)
    hidden["own"] = blocks_of(held(hidden["own"], last[0]))
    if chips > 2:
        last.extend(sent)
        project_far_patched(lab)
    project_near(lab)
    project_own(late)

    return add_up(*parts, 2)


def solution(mesh):
    n_row, n_col = mesh.shape["row"], mesh.shape["col"]
    placed = (
        P("row", "col"),
        P("row", "col"),
        P(),
        P("col", "row"),
        P("col", "row"),
        P("row", "col"),
    )

    def on_device(*args):
        patch_mask = args[2]
        tok = patch_mask.shape[0]
        chip_tok = 2 * args[0].shape[0]
        cap_own, cap_rest = capacities(tok, chip_tok, False)
        per_chip = jnp.sum((patch_mask != 1).astype(I32).reshape(tok // chip_tok, chip_tok), axis=1)
        fits = (jnp.max(per_chip) <= cap_own) & (jnp.sum(per_chip) - jnp.min(per_chip) <= cap_rest)
        outs = body(False, n_row, n_col, *args)
        return lax.cond(fits, lambda *a: outs, lambda *a: body(True, n_row, n_col, *a), *args)

    return jax.shard_map(
        on_device,
        mesh=mesh,
        in_specs=placed,
        out_specs=(P("row", "col"), P("row", "col")),
        check_vma=False,
    )
```
